256 devices in a mesh: patch: 64 (over y, x, z_lo), head: 4 (over z_hi, core).
Axes of the slice: x: 4, y: 4, z: 8 (z_hi: 2, z_lo: 4; z = z_hi * 4 + z_lo), core: 2. Of those that a mesh axis runs over, the one named last changes fastest.
Arguments:
- image_tokens: bfloat16 [16384, 3072], P(('patch', 'head')), may hold values from -6 to 6
- shift: float32 [3072], replicated, may hold values from -4 to 4
- scale: float32 [3072], replicated, may hold values from -3 to 3
- w_query: bfloat16 [3072, 1536], P(None, 'head'), may hold values from -0.109375 to 0.109375
- w_key: bfloat16 [3072, 1536], P(None, 'head'), may hold values from -0.109375 to 0.109375
- w_value: bfloat16 [3072, 1536], P(None, 'head'), may hold values from -0.109375 to 0.109375
- q_gain: float32 [128], replicated, may hold values from 1 to 4
- k_gain: float32 [128], replicated, may hold values from 1 to 4
- stale_keys: bfloat16 [16384, 1536], P('patch', 'head'), may hold values from -120 to 120
- stale_values: bfloat16 [16384, 1536], P('patch', 'head'), may hold values from -6 to 6
- text_keys: bfloat16 [512, 1536], P(None, 'head'), may hold values from -14 to 14
- text_values: bfloat16 [512, 1536], P(None, 'head'), may hold values from -6 to 6
Outputs:
- attended: bfloat16 [16384, 1536], P(('patch', 'head'))
- fresh_keys: bfloat16 [16384, 1536], P('patch', 'head')
- fresh_values: bfloat16 [16384, 1536], P('patch', 'head')
The draws below stay inside these ranges and needn't reach their ends.
All inputs are finite; a program needn't handle non-finite values.
Results may differ from the reference program's by a relative error of at most 0.022.
The reference program's roundings to bfloat16 on the way (of `modulated`, `queries`, `key_rows` and `rounded`) count: a program that leaves them out, or rounds other values in their place, can miss the bound.
Values may be sent and summed in bfloat16 or wider, within the bound.
No kernel may reach another device: no remote copies, remote signals or barrier semaphores. Data moves between devices by JAX's collectives and lax.ppermute only.
A program may use at most 128 MiB of HBM per device.

```python
import math
import jax
import jax.numpy as jnp
from jax import lax

D = 3072
HEADS = 12
HDIM = 128
TEXT = 512
SIDE = 128
IMG = 16384
N_PATCH = 64


def draw_stale_keys(key, part):
    key = jax.random.fold_in(key, 11)
    main_key = jax.random.fold_in(key, 0)
    values = 2.3 * jax.random.normal(main_key, (IMG, HEADS * HDIM), jnp.float32)
    values = jnp.clip(values, -9.0, 9.0)
    return values.astype(jnp.bfloat16)


def level_of(stream_key, extent, shards, least, high):
    level = 1.0
    for position, shards_of in shards:
        steps = jax.random.uniform(jax.random.fold_in(jax.random.fold_in(stream_key, 6), position), (shards_of,), jnp.float32, least / len(shards), high / len(shards))
        level = level * jnp.repeat(jnp.exp(steps), extent[position] // shards_of).reshape((-1,) + (1,) * (len(extent) - 1 - position))
    return level


def bell_draw(key, dims, deviation, reach, shards=(), kind=jnp.bfloat16):
    level = level_of(key, dims, shards, -0.22, 0.18) if shards else 1.0
    entries = jax.random.normal(key, dims, jnp.float32) * deviation * level
    return jnp.minimum(jnp.maximum(entries, -reach), reach).astype(kind)


def setup_inputs(seed: int = 0) -> dict:
    splits = jax.random.split(jax.random.key(seed), 13)
    image_tokens = bell_draw(splits[0], (IMG, D), 1.0, 6.0, ((0, 256),))
    shift = bell_draw(splits[1], (D,), 0.5, 4.0, (), jnp.float32)
    scale = bell_draw(splits[2], (D,), 0.3, 3.0, (), jnp.float32)
    w_query = bell_draw(splits[3], (D, HEADS * HDIM), D ** -0.5, 0.109375, ((1, 4),))
    w_key = bell_draw(splits[4], (D, HEADS * HDIM), D ** -0.5, 0.109375, ((1, 4),))
    w_value = bell_draw(splits[5], (D, HEADS * HDIM), D ** -0.5, 0.109375, ((1, 4),))
    q_gain = jnp.clip(jnp.exp(jax.random.uniform(splits[6], (HDIM,), jnp.float32, math.log(1.0), math.log(4.0))), 1.0, 4.0)
    k_gain = jnp.clip(jnp.exp(jax.random.uniform(splits[7], (HDIM,), jnp.float32, math.log(1.0), math.log(4.0))), 1.0, 4.0)
    stale_keys = draw_stale_keys(jax.random.fold_in(splits[12], 71), 0)
    stale_values = bell_draw(splits[9], (IMG, HEADS * HDIM), 1.0, 6.0, ((0, 64), (1, 4)))
    text_keys = bell_draw(splits[10], (TEXT, HEADS * HDIM), 2.3, 14.0, ((1, 4),))
    text_values = bell_draw(splits[11], (TEXT, HEADS * HDIM), 1.0, 6.0, ((1, 4),))
    return dict(image_tokens=image_tokens, shift=shift, scale=scale, w_query=w_query, w_key=w_key, w_value=w_value, q_gain=q_gain, k_gain=k_gain, stale_keys=stale_keys, stale_values=stale_values, text_keys=text_keys, text_values=text_values)


theta_base = 10000.0
norm_eps = 1e-06

def modulate(rows, shift, scale):
    values = rows.astype(jnp.float32)
    centred = values - lax.optimization_barrier(jnp.mean(values, -1, keepdims=True))
    variance = lax.optimization_barrier(jnp.mean(centred * centred, -1, keepdims=True))
    normed = centred * lax.rsqrt(variance + norm_eps)
    return (normed * (1.0 + scale) + shift).astype(jnp.bfloat16)

def rotary(positions, head_size):
    half = head_size // 2
    first = half // 8
    row_count = (half - first) // 2
    col_count = half - first - row_count
    index = jnp.arange(half).astype(jnp.float32)
    grid_row = (positions // SIDE).astype(jnp.float32)[:, None]
    grid_col = (positions % SIDE).astype(jnp.float32)[:, None]
    row_freq = jnp.power(theta_base, -(index - first) / row_count)
    col_freq = jnp.power(theta_base, -(index - first - row_count) / col_count)
    angle = jnp.where(index < first, 0.0 * grid_row, jnp.where(index < first + row_count, grid_row * row_freq, grid_col * col_freq))
    return (jnp.cos(angle), jnp.sin(angle))

def norm_rotate(projected, gain, positions, head_size):
    count = projected.shape[0]
    heads_view = projected.reshape(count, -1, head_size)
    squares = lax.optimization_barrier(jnp.mean(heads_view * heads_view, -1, keepdims=True))
    normed = heads_view * lax.rsqrt(squares + norm_eps) * gain
    cosine, sine = rotary(positions, head_size)
    half = head_size // 2
    lower = normed[..., :half]
    upper = normed[..., half:]
    cosine = cosine[:, None, :]
    sine = sine[:, None, :]
    turned = jnp.concatenate([lower * cosine - upper * sine, lower * sine + upper * cosine], -1)
    return turned.reshape(count, -1)

def reference(image_tokens, shift, scale, w_query, w_key, w_value, q_gain, k_gain, stale_keys, stale_values, text_keys, text_values):
    modulated = modulate(image_tokens, shift, scale)
    positions = jnp.arange(IMG).astype(jnp.int32)
    queries = norm_rotate(jnp.dot(modulated, w_query, preferred_element_type=jnp.float32), q_gain, positions, HDIM).astype(jnp.bfloat16)
    fresh_keys = norm_rotate(jnp.dot(modulated, w_key, preferred_element_type=jnp.float32), k_gain, positions, HDIM).astype(jnp.bfloat16)
    fresh_values = jnp.dot(modulated, w_value, preferred_element_type=jnp.float32).astype(jnp.bfloat16)
    block_rows = IMG // N_PATCH
    factor = 1.0 / math.sqrt(HDIM)

    def one_block(index):
        start = (index * block_rows).astype(jnp.int32)
        query_rows = lax.dynamic_slice_in_dim(queries, start, block_rows, 0)
        own_keys = lax.dynamic_slice_in_dim(fresh_keys, start, block_rows, 0)
        own_values = lax.dynamic_slice_in_dim(fresh_values, start, block_rows, 0)
        key_rows = jnp.concatenate([text_keys, lax.dynamic_update_slice_in_dim(stale_keys, own_keys, start, 0)], 0)
        value_rows = jnp.concatenate([text_values, lax.dynamic_update_slice_in_dim(stale_values, own_values, start, 0)], 0)
        query_view = query_rows.astype(jnp.float32).reshape(block_rows, HEADS, HDIM)
        key_view = key_rows.astype(jnp.float32).reshape(-1, HEADS, HDIM)
        value_view = value_rows.astype(jnp.float32).reshape(-1, HEADS, HDIM)
        scores = jnp.einsum('qhd,khd->qhk', query_view, key_view) * factor
        largest = lax.optimization_barrier(jnp.max(scores, -1, keepdims=True))
        weights = jnp.exp(scores - largest)
        totals = lax.optimization_barrier(jnp.sum(weights, -1))
        rounded = lax.optimization_barrier(weights.astype(jnp.bfloat16)).astype(jnp.float32)
        summed = jnp.einsum('qhk,khd->qhd', rounded, value_view)
        return (summed / totals[:, :, None]).reshape(block_rows, HEADS * HDIM).astype(jnp.bfloat16)
    attended = lax.map(one_block, jnp.arange(N_PATCH).astype(jnp.int32)).reshape(IMG, HEADS * HDIM)
    return (attended, fresh_keys, fresh_values)
```

```python
import functools
import math

import jax
import jax.numpy as jnp
from jax import lax
from jax.experimental import pallas as pl
from jax.experimental.pallas import tpu as pltpu
from jax.sharding import PartitionSpec as P

SIDE = 128
THETA = 10000.0
EPS = 1e-06
HS = 128
LOG2E = math.log2(math.e)
VMEM = pl.BlockSpec(memory_space=pltpu.VMEM)
SMEM = pl.BlockSpec(memory_space=pltpu.SMEM)
HBM = pl.BlockSpec(memory_space=pl.ANY)
LIMIT = 48 * 2**20


def patch_permute(move):
    pairs = []
    for y in range(4):
        for x in range(4):
            for z in range(4):
                ty, tx, tz = move(y, x, z)
                pairs.append(((y * 4 + x) * 4 + z, (ty * 4 + tx) * 4 + tz))
    return lambda v: lax.ppermute(v, "patch", pairs)


def along_x(d):
    return patch_permute(lambda y, x, z: (y, (x + d) % 4, z))


def along_y(d):
    return patch_permute(lambda y, x, z: ((y + d) % 4, x, z))


def across_z(bits):
    return patch_permute(lambda y, x, z: (y, x, z ^ bits))


def across_head(bits):
    return lambda v: lax.ppermute(v, "head", [(h, h ^ bits) for h in range(4)])


def ring(v, along):
    left = along(1)(v)
    right = along(3)(v)
    half = v.shape[0] // 2
    far_a = along(1)(left[:half])
    far_b = along(3)(right[half:])
    return jnp.concatenate([v, left, right, far_a, far_b], 0)


def rotary(positions):
    half = HS // 2
    first = half // 8
    row_count = (half - first) // 2
    col_count = half - first - row_count
    index = jnp.arange(half).astype(jnp.float32)
    grid_row = (positions // SIDE).astype(jnp.float32)[:, None]
    grid_col = (positions % SIDE).astype(jnp.float32)[:, None]
    row_freq = jnp.power(THETA, -(index - first) / row_count)
    col_freq = jnp.power(THETA, -(index - first - row_count) / col_count)
    angle = jnp.where(
        index < first,
        0.0 * grid_row,
        jnp.where(index < first + row_count, grid_row * row_freq, grid_col * col_freq),
    )
    cosine, sine = jnp.cos(angle), jnp.sin(angle)
    return jnp.concatenate([cosine, cosine], 1), jnp.concatenate([-sine, sine], 1)


def project_kernel(
    h_ref, a0, a1, a2, a3, shift, scale, wq, wk, wv, qg, kg, cos, sin, q_out, k_out, v_out, mod, wbuf, sems
):
    copies = [
        pltpu.make_async_copy(w, wbuf.at[i], sems.at[i]) for i, w in enumerate((wq, wk, wv))
    ]
    for c in copies:
        c.start()
    for j, a in enumerate((a0, a1, a2, a3)):
        values = a[...].astype(jnp.float32)
        centred = values - jnp.mean(values, -1, keepdims=True)
        variance = jnp.mean(centred * centred, -1, keepdims=True)
        normed = centred * lax.rsqrt(variance + EPS)
        mod[j * 64 : j * 64 + 64, :] = (normed * (1.0 + scale[...]) + shift[...]).astype(jnp.bfloat16)

    def norm_rotate(full, gain, store):
        for n in range(full.shape[1] // HS):
            u = full[:, n * HS : n * HS + HS]
            squares = jnp.mean(u * u, -1, keepdims=True)
            u = u * lax.rsqrt(squares + EPS) * gain[...]
            turned = u * cos[...] + pltpu.roll(u, HS // 2, 1) * sin[...]
            store(n, turned.astype(jnp.bfloat16))

    h = h_ref[0]

    def ordered(out, n, block):
        for j in range(4):
            row = pl.multiple_of((h ^ j) * 64, 64)
            out[pl.ds(row, 64), n * HS : n * HS + HS] = block[j * 64 : j * 64 + 64]

    def store_q(n, block):
        q_out[:, n * HS : n * HS + HS] = block

    copies[0].wait()
    norm_rotate(jnp.dot(mod[...], wbuf[0], preferred_element_type=jnp.float32), qg, store_q)
    copies[1].wait()
    norm_rotate(
        jnp.dot(mod[...], wbuf[1], preferred_element_type=jnp.float32), kg, functools.partial(ordered, k_out)
    )
    copies[2].wait()
    values = jnp.dot(mod[...], wbuf[2], preferred_element_type=jnp.float32).astype(jnp.bfloat16)
    for n in range(values.shape[1] // HS):
        ordered(v_out, n, values[:, n * HS : n * HS + HS])


def project(h, pieces, shift, scale, wq, wk, wv, qg, kg, cos, sin):
    rows, width = 4 * pieces[0].shape[0], wq.shape[1]
    out = jax.ShapeDtypeStruct((rows, width), jnp.bfloat16)
    return pl.pallas_call(
        project_kernel,
        out_shape=[out] * 3,
        in_specs=[SMEM] + [VMEM] * 6 + [HBM] * 3 + [VMEM] * 4,
        out_specs=[VMEM] * 3,
        scratch_shapes=[
            pltpu.VMEM((rows, wq.shape[0]), jnp.bfloat16),
            pltpu.VMEM((3,) + wq.shape, jnp.bfloat16),
            pltpu.SemaphoreType.DMA((3,)),
        ],
        compiler_params=pltpu.CompilerParams(vmem_limit_bytes=LIMIT),
        cost_estimate=pl.CostEstimate(
            flops=2 * rows * wq.size * 3, bytes_accessed=6 * wq.size, transcendentals=0
        ),
        name="project",
    )(h, *pieces, shift[None], scale[None], wq, wk, wv, qg[None], kg[None], cos, sin)


def attend_kernel(q_ref, *refs, tiles, count):
    k_refs, v_refs = refs[:count], refs[count : 2 * count]
    o_ref, l_ref = refs[2 * count :]
    factor = LOG2E / math.sqrt(HS)
    rows, width = q_ref.shape
    lane = lax.broadcasted_iota(jnp.int32, (rows, HS), 1)
    logs = jnp.zeros((rows, HS), jnp.float32)
    for n in range(width // HS):
        cols = slice(n * HS, n * HS + HS)
        q = q_ref[:, cols]
        top = acc = None
        for which, start, size in tiles:
            k = k_refs[which][start : start + size, cols]
            v = v_refs[which][start : start + size, cols]
            s = lax.dot_general(q, k, (((1,), (1,)), ((), ())), preferred_element_type=jnp.float32)
            new = jnp.max(s, -1, keepdims=True)
            if top is not None:
                new = jnp.maximum(top, new)
            p = jnp.exp2((s - new) * factor).astype(jnp.bfloat16)
            part = jnp.dot(p, jnp.concatenate([v, jnp.ones_like(v)], 1), preferred_element_type=jnp.float32)
            acc = part if top is None else acc * jnp.exp2((top - new) * factor) + part
            top = new
        total = acc[:, HS : HS + 1]
        o_ref[:, cols] = (acc[:, :HS] / total).astype(o_ref.dtype)
        logs = jnp.where(lane == n, top * factor + jnp.log2(total), logs)
    l_ref[...] = logs.T[:8]


def attend(q, keys, values, tiles, dtype, name):
    rows, width = q.shape
    span = sum(t[2] for t in tiles)
    return pl.pallas_call(
        functools.partial(attend_kernel, tiles=tiles, count=len(keys)),
        out_shape=[
            jax.ShapeDtypeStruct((rows, width), dtype),
            jax.ShapeDtypeStruct((8, rows), jnp.float32),
        ],
        in_specs=[VMEM] * (1 + 2 * len(keys)),
        out_specs=[VMEM] * 2,
        compiler_params=pltpu.CompilerParams(vmem_limit_bytes=LIMIT),
        cost_estimate=pl.CostEstimate(
            flops=8 * rows * width * span, bytes_accessed=4 * span * width, transcendentals=rows * span * 3
        ),
        name=name,
    )(q, *keys, *values)


def combine_kernel(o0, l0, o1, l1, o2, l2, o3, l3, near, far):
    rows, width = o0.shape
    logs = [l[...] for l in (l0, l1, l2, l3)]
    top = functools.reduce(jnp.maximum, logs)
    weights = [jnp.exp2(l - top) for l in logs]
    total = functools.reduce(jnp.add, weights)
    pad = jnp.zeros((HS - 8, rows), jnp.float32)
    weights = [jnp.concatenate([w / total, pad], 0).T for w in weights]
    half = rows // 2
    for n in range(width // HS):
        cols = slice(n * HS, n * HS + HS)
        out = functools.reduce(
            jnp.add,
            [w[:, n : n + 1] * o[:, cols].astype(jnp.float32) for w, o in zip(weights, (o0, o1, o2, o3))],
        ).astype(jnp.bfloat16)
        near[:, cols] = out[:half]
        far[:, cols] = out[half:]


def combine(parts):
    rows, width = parts[0][0].shape
    out = jax.ShapeDtypeStruct((rows // 2, width), jnp.bfloat16)
    return pl.pallas_call(
        combine_kernel,
        out_shape=[out, out],
        in_specs=[VMEM] * 8,
        out_specs=[VMEM] * 2,
        name="combine",
    )(*[a for part in parts for a in part])


def place_kernel(h_ref, near, far, crossed, out):
    width = near.shape[1]
    h = h_ref[0]
    pieces = (near[:64], crossed[:64], far[:64], crossed[64:])
    for j, piece in enumerate(pieces):
        out[:, pl.ds(pl.multiple_of((h ^ j) * width, HS), width)] = piece


def place(h, near, far, crossed):
    return pl.pallas_call(
        place_kernel,
        out_shape=jax.ShapeDtypeStruct((64, 4 * near.shape[1]), jnp.bfloat16),
        in_specs=[SMEM] + [VMEM] * 3,
        out_specs=VMEM,
        name="place",
    )(h, near, far, crossed)


def local(
    image_tokens,
    shift,
    scale,
    w_query,
    w_key,
    w_value,
    q_gain,
    k_gain,
    stale_keys,
    stale_values,
    text_keys,
    text_values,
):
    rows = stale_keys.shape[0]
    piece = image_tokens.shape[0]
    head = lax.axis_index("head").astype(jnp.int32)
    h = head[None]
    order = (head ^ jnp.arange(4, dtype=jnp.int32))[:, None] * piece + jnp.arange(piece, dtype=jnp.int32)
    cos, sin = rotary(lax.axis_index("patch") * rows + order.reshape(-1))

    far_rows = across_head(2)(image_tokens)
    pieces = [image_tokens, across_head(1)(image_tokens), far_rows, across_head(1)(far_rows)]
    keys = ring(ring(stale_keys, along_x), along_y)
    values = ring(ring(stale_values, along_y), along_x)
    values = reorder(values, rows)
    queries, fresh_keys, fresh_values = project(
        h, pieces, shift, scale, w_query, w_key, w_value, q_gain, k_gain, cos, sin
    )

    step = 1024
    tiles = [(0, i, step) for i in range(0, keys.shape[0], step)]
    returned = []
    for bits in (1, 2, 3):
        part = attend(across_z(bits)(queries), [keys], [values], tiles, jnp.bfloat16, "attend_other")
        returned.append([across_z(bits)(a) for a in part])
    text = text_keys.shape[0]
    own_tiles = [(0, 0, text), (1, 0, rows), (2, rows, step - rows)] + [(2, s, n) for _, s, n in tiles[1:]]
    own = attend(
        queries,
        [text_keys, fresh_keys, keys],
        [text_values, fresh_values, values],
        own_tiles,
        jnp.float32,
        "attend_own",
    )
    near, far = combine([own] + returned)
    far = across_head(2)(far)
    crossed = across_head(1)(jnp.concatenate([near[piece:], far[piece:]], 0))
    attended = place(h, near, far, crossed)
    return (attended, fresh_keys, fresh_values)


def reorder(values, rows):
    grid = values.reshape(4, 4, rows, values.shape[1])
    return jnp.swapaxes(grid, 0, 1).reshape(values.shape)


def solution(mesh):
    placed = (
        P(("patch", "head"), None),
        P(),
        P(),
        P(None, "head"),
        P(None, "head"),
        P(None, "head"),
        P(),
        P(),
        P("patch", "head"),
        P("patch", "head"),
        P(None, "head"),
        P(None, "head"),
    )
    return jax.shard_map(
        local,
        mesh=mesh,
        in_specs=placed,
        out_specs=(P(("patch", "head"), None), P("patch", "head"), P("patch", "head")),
        check_vma=False,
    )
```

```python
import functools
import math

import jax
import jax.numpy as jnp
from jax import lax
from jax.experimental import pallas as pl
from jax.experimental.pallas import tpu as pltpu
from jax.sharding import PartitionSpec as P

SIDE = 128
THETA = 10000.0
EPS = 1e-06
HS = 128
LOG2E = math.log2(math.e)
VMEM = pl.BlockSpec(memory_space=pltpu.VMEM)
SMEM = pl.BlockSpec(memory_space=pltpu.SMEM)
ANY = pl.BlockSpec(memory_space=pl.ANY)
HBM = pl.BlockSpec(memory_space=pltpu.HBM)
PACK = 4 * 2**20
PROJECT = 20 * 2**20


def patch_permute(move):
    pairs = []
    for y in range(4):
        for x in range(4):
            for z in range(4):
                ty, tx, tz = move(y, x, z)
                pairs.append(((y * 4 + x) * 4 + z, (ty * 4 + tx) * 4 + tz))
    return lambda v: lax.ppermute(v, "patch", pairs)


def along_x(d):
    return patch_permute(lambda y, x, z: (y, (x + d) % 4, z))


def along_y(d):
    return patch_permute(lambda y, x, z: ((y + d) % 4, x, z))


def across_z(bits):
    return patch_permute(lambda y, x, z: (y, x, z ^ bits))


def across_head(bits):
    return lambda v: lax.ppermute(v, "head", [(h, h ^ bits) for h in range(4)])


def rotary(positions):
    half = HS // 2
    first = half // 8
    row_count = (half - first) // 2
    col_count = half - first - row_count
    index = jnp.arange(half).astype(jnp.float32)
    grid_row = (positions // SIDE).astype(jnp.float32)[:, None]
    grid_col = (positions % SIDE).astype(jnp.float32)[:, None]
    row_freq = jnp.power(THETA, -(index - first) / row_count)
    col_freq = jnp.power(THETA, -(index - first - row_count) / col_count)
    angle = jnp.where(
        index < first,
        0.0 * grid_row,
        jnp.where(index < first + row_count, grid_row * row_freq, grid_col * col_freq),
    )
    cosine, sine = jnp.cos(angle), jnp.sin(angle)
    return jnp.concatenate([cosine, cosine], 1), jnp.concatenate([-sine, sine], 1)


def project_kernel(
    h_ref, a0, a1, a2, a3, shift, scale, wq, wk, wv, qg, kg, cos, sin, q_out, k_out, v_out, mod
):
    for j, a in enumerate((a0, a1, a2, a3)):
        values = a[...].astype(jnp.float32)
        centred = values - jnp.mean(values, -1, keepdims=True)
        variance = jnp.mean(centred * centred, -1, keepdims=True)
        normed = centred * lax.rsqrt(variance + EPS)
        mod[j * 64 : j * 64 + 64, :] = (normed * (1.0 + scale[...]) + shift[...]).astype(jnp.bfloat16)

    def norm_rotate(full, gain, store):
        for n in range(full.shape[1] // HS):
            u = full[:, n * HS : n * HS + HS]
            squares = jnp.mean(u * u, -1, keepdims=True)
            u = u * lax.rsqrt(squares + EPS) * gain[...]
            turned = u * cos[...] + pltpu.roll(u, HS // 2, 1) * sin[...]
            store(n, turned.astype(jnp.bfloat16))

    h = h_ref[0]

    def ordered(out, n, block):
        for j in range(4):
            row = pl.multiple_of((h ^ j) * 64, 64)
            out[pl.ds(row, 64), n * HS : n * HS + HS] = block[j * 64 : j * 64 + 64]

    def store_q(n, block):
        q_out[:, n * HS : n * HS + HS] = block

    norm_rotate(jnp.dot(mod[...], wq[...], preferred_element_type=jnp.float32), qg, store_q)
    norm_rotate(
        jnp.dot(mod[...], wk[...], preferred_element_type=jnp.float32), kg, functools.partial(ordered, k_out)
    )
    values = jnp.dot(mod[...], wv[...], preferred_element_type=jnp.float32).astype(jnp.bfloat16)
    for n in range(values.shape[1] // HS):
        ordered(v_out, n, values[:, n * HS : n * HS + HS])


def project(h, pieces, shift, scale, wq, wk, wv, qg, kg, cos, sin):
    rows, width = 4 * pieces[0].shape[0], wq.shape[1]
    out = jax.ShapeDtypeStruct((rows, width), jnp.bfloat16)
    return pl.pallas_call(
        project_kernel,
        out_shape=[out] * 3,
        in_specs=[SMEM] + [VMEM] * 13,
        out_specs=[VMEM] * 3,
        scratch_shapes=[
            pltpu.VMEM((rows, wq.shape[0]), jnp.bfloat16),
        ],
        compiler_params=pltpu.CompilerParams(vmem_limit_bytes=PROJECT),
        name="project",
    )(h, *pieces, shift[None], scale[None], wq, wk, wv, qg[None], kg[None], cos, sin)


def pack_kernel(k, v, a, b, sems):
    half, width = a.shape[0], k.shape[1]
    copies = []
    for i, out in enumerate((a, b)):
        for j, source in enumerate((k, v)):
            copies.append(
                pltpu.make_async_copy(
                    source.at[i * half : i * half + half],
                    out.at[:, j * width : j * width + width],
                    sems.at[2 * i + j],
                )
            )
    for c in copies:
        c.start()
    for c in copies:
        c.wait()


def pack(k, v):
    out = jax.ShapeDtypeStruct((k.shape[0] // 2, 2 * k.shape[1]), k.dtype)
    return pl.pallas_call(
        pack_kernel,
        out_shape=[out, out],
        in_specs=[HBM] * 2,
        out_specs=[VMEM] * 2,
        scratch_shapes=[pltpu.SemaphoreType.DMA((4,))],
        compiler_params=pltpu.CompilerParams(vmem_limit_bytes=PACK),
        cost_estimate=pl.CostEstimate(flops=0, bytes_accessed=4 * 2**20, transcendentals=0),
        name="pack",
    )(k, v)


def join_kernel(*refs, groups, count):
    sources, outs = refs[:count], refs[-len(groups) :]
    for out, group in zip(outs, groups):
        at = 0
        for i, start, size in group:
            out[at : at + size] = sources[i][start : start + size]
            at += size


def join(sources, groups, after, name):
    return pl.pallas_call(
        functools.partial(join_kernel, groups=groups, count=len(sources)),
        out_shape=[
            jax.ShapeDtypeStruct((sum(g[2] for g in group), sources[group[0][0]].shape[1]), jnp.bfloat16)
            for group in groups
        ],
        in_specs=[VMEM] * len(sources) + [ANY] * len(after),
        out_specs=[VMEM] * len(groups),
        compiler_params=pltpu.CompilerParams(vmem_limit_bytes=8 * 2**20),
        cost_estimate=pl.CostEstimate(flops=0, bytes_accessed=2 * 2**20, transcendentals=0),
        name=name,
    )(*sources, *after)


def touch_kernel(*refs):
    refs[-1][...] = jnp.zeros_like(refs[-1])


def touch(arrays, after):
    return pl.pallas_call(
        touch_kernel,
        out_shape=jax.ShapeDtypeStruct((16, HS), jnp.bfloat16),
        in_specs=[VMEM] * len(arrays) + [ANY] * len(after),
        out_specs=VMEM,
        compiler_params=pltpu.CompilerParams(vmem_limit_bytes=2**20),
        name="touch",
    )(*arrays, *after)


def attend_kernel(q_ref, *refs, tiles, count, resumed, outputs):
    sources, outs = refs[:count], refs[-outputs:]
    factor = LOG2E / math.sqrt(HS)
    rows, width = q_ref.shape
    heads = width // HS
    lane = lax.broadcasted_iota(jnp.int32, (rows, HS), 1)
    lanes = jnp.zeros((rows, HS), jnp.float32)
    last = outputs == 1

    def load(parts):
        return jnp.concatenate([sources[i][start : start + size, c : c + HS] for i, start, size, c in parts], 0)

    for n in range(heads):
        cols = slice(n * HS, n * HS + HS)
        q = q_ref[:, cols]
        top = acc = None
        if resumed:
            sums, tops = refs[count], refs[count + 1]
            top = tops[:, n : n + 1]
            total = jnp.broadcast_to(tops[:, 4 + n : 5 + n], (rows, HS))
            acc = jnp.concatenate([sums[:, cols], total], 1)
        for tile in tiles:
            k = load([(ki, start, size, n * HS) for ki, vi, start, size in tile])
            v = load([(vi, start, size, n * HS + (width if vi == ki else 0)) for ki, vi, start, size in tile])
            s = lax.dot_general(q, k, (((1,), (1,)), ((), ())), preferred_element_type=jnp.float32)
            new = jnp.max(s, -1, keepdims=True)
            if top is not None:
                new = jnp.maximum(top, new)
            p = jnp.exp2((s - new) * factor).astype(jnp.bfloat16)
            part = jnp.dot(p, jnp.concatenate([v, jnp.ones_like(v)], 1), preferred_element_type=jnp.float32)
            acc = part if top is None else acc * jnp.exp2((top - new) * factor) + part
            top = new
        total = acc[:, HS : HS + 1]
        if not last:
            outs[0][:, cols] = acc[:, :HS]
            lanes = jnp.where(lane == n, top, jnp.where(lane == 4 + n, total, lanes))
        else:
            outs[0][:rows, cols] = (acc[:, :HS] / total).astype(jnp.bfloat16)
            log = top * factor + jnp.log2(total)
            for t in range(3):
                term = log.astype(jnp.bfloat16).astype(jnp.float32)
                lanes = jnp.where(lane == 4 * t + n, term, lanes)
                log = log - term
    if not last:
        outs[1][...] = lanes
    else:
        outs[0][rows:, :rows] = lanes.T[:16].astype(jnp.bfloat16)
        outs[0][rows:, rows:] = jnp.zeros((16, width - rows), jnp.bfloat16)


def attend(q, sources, segments, state, last, after, name):
    rows, width = q.shape
    tiles, span = [[]], 0
    for segment in segments:
        if sum(t[3] for t in tiles[-1]) + segment[3] > 1152:
            tiles.append([])
        tiles[-1].append(segment)
        span += segment[3]
    if last:
        out_shape = [jax.ShapeDtypeStruct((rows + 16, width), jnp.bfloat16)]
    else:
        out_shape = [
            jax.ShapeDtypeStruct((rows, width), jnp.float32),
            jax.ShapeDtypeStruct((rows, HS), jnp.float32),
        ]
    state = list(state or ())
    return pl.pallas_call(
        functools.partial(
            attend_kernel, tiles=tiles, count=len(sources), resumed=bool(state), outputs=len(out_shape)
        ),
        out_shape=out_shape,
        in_specs=[VMEM] * (1 + len(sources) + len(state)) + [ANY] * len(after),
        out_specs=[VMEM] * len(out_shape),
        compiler_params=pltpu.CompilerParams(vmem_limit_bytes=16 * 2**20),
        cost_estimate=pl.CostEstimate(
            flops=8 * rows * width * span, bytes_accessed=4 * span * width, transcendentals=rows * span * 3
        ),
        name=name,
    )(q, *sources, *state, *after)


def combine_kernel(own, tops, o1, o2, o3, mine, near, far):
    rows, width = own.shape
    factor = LOG2E / math.sqrt(HS)
    state = tops[...].T
    totals = state[4:8]
    heads = width // HS
    first = lax.broadcasted_iota(jnp.int32, totals.shape, 0) < heads
    totals = jnp.where(first, totals, 1.0)
    logs = [state[:4] * factor + jnp.log2(totals)]
    for o in (o1, o2, o3):
        terms = o[rows:, :rows].astype(jnp.float32)
        logs.append(terms[:4] + terms[4:8] + terms[8:12])
    top = functools.reduce(jnp.maximum, logs)
    weights = [jnp.exp2(l - top) for l in logs]
    total = functools.reduce(jnp.add, weights)
    pad = jnp.zeros((HS - 4, rows), jnp.float32)
    weights = [w / total for w in weights]
    weights[0] = weights[0] / totals
    weights = [jnp.concatenate([w, pad], 0).T for w in weights]
    for n in range(width // HS):
        cols = slice(n * HS, n * HS + HS)
        out = functools.reduce(
            jnp.add,
            [w[:, n : n + 1] * o[:rows, cols].astype(jnp.float32) for w, o in zip(weights, (own, o1, o2, o3))],
        ).astype(jnp.bfloat16)
        mine[:, cols] = out[:64]
        near[:, cols] = out[64:128]
        far[:, cols] = out[128:]


def combine(own, others):
    rows, width = own[0].shape
    piece = jax.ShapeDtypeStruct((rows // 4, width), jnp.bfloat16)
    return pl.pallas_call(
        combine_kernel,
        out_shape=[piece, piece, jax.ShapeDtypeStruct((rows // 2, width), jnp.bfloat16)],
        in_specs=[VMEM] * 5,
        out_specs=[VMEM] * 3,
        compiler_params=pltpu.CompilerParams(vmem_limit_bytes=8 * 2**20),
        name="combine",
    )(*own, *others)


def place_kernel(h_ref, mine, near, far, far_near, out):
    width = near.shape[1]
    h = h_ref[0]
    pieces = (mine[...], near[...], far[:64], far_near[...])
    for j, piece in enumerate(pieces):
        out[:, pl.ds(pl.multiple_of((h ^ j) * width, HS), width)] = piece


def place(h, mine, near, far, far_near):
    return pl.pallas_call(
        place_kernel,
        out_shape=jax.ShapeDtypeStruct((64, 4 * near.shape[1]), jnp.bfloat16),
        in_specs=[SMEM] + [VMEM] * 4,
        out_specs=VMEM,
        compiler_params=pltpu.CompilerParams(vmem_limit_bytes=4 * 2**20),
        name="place",
    )(h, mine, near, far, far_near)


def local(
    image_tokens,
    shift,
    scale,
    w_query,
    w_key,
    w_value,
    q_gain,
    k_gain,
    stale_keys,
    stale_values,
    text_keys,
    text_values,
):
    rows = stale_keys.shape[0]
    piece = image_tokens.shape[0]
    head = lax.axis_index("head").astype(jnp.int32)
    h = head[None]
    order = (head ^ jnp.arange(4, dtype=jnp.int32))[:, None] * piece + jnp.arange(piece, dtype=jnp.int32)
    cos, sin = rotary(lax.axis_index("patch") * rows + order.reshape(-1))

    far_rows = across_head(2)(image_tokens)
    beside_rows = across_head(1)(image_tokens)
    pieces = [image_tokens, beside_rows, far_rows, across_head(1)(far_rows)]

    half = rows // 2
    packed = pack(stale_keys, stale_values)
    ways = (along_x, along_y)
    beside = [along(d)(v) for v, along in zip(packed, ways) for d in (1, 3)]
    again = join(packed, [[(0, 0, half)], [(1, 0, half)]], beside, "hold_first")
    across = [along(2)(v) for v, along in zip(again, ways)]
    touched = touch([w_key, w_value], [again[0]])
    near_lists = join(
        [packed[0], *beside[:2], across[0], packed[1], *beside[2:], across[1]],
        [[(4 * g + i, 0, half) for i in range(4)] for g in range(2)],
        [touched],
        "join_lines",
    )
    next_lists = []
    for v, along in zip(near_lists, (along_y, along_x)):
        next_lists += [along(1)(v), along(3)(v)]

    queries, fresh_keys, fresh_values = project(
        h, pieces, shift, scale, w_query, w_key, w_value, q_gain, k_gain, cos, sin
    )
    asked = {3: across_z(3)(queries), 2: across_z(2)(queries)}

    text = text_keys.shape[0]
    own = attend(
        queries,
        list(near_lists) + [text_keys, text_values, fresh_keys, fresh_values],
        [(2, 3, 0, text), (4, 5, 0, rows), (0, 0, half, 3 * half), (1, 1, half, 3 * half)],
        None,
        False,
        [],
        "attend_own_near",
    )
    halves = join(
        next_lists, [[(i, (i % 2) * 2 * half, 2 * half)] for i in range(4)], [own[1], asked[3]], "join_halves"
    )
    far_lists = []
    for i, along in enumerate((along_y, along_y, along_x, along_x)):
        far_lists.append(along((1, 3)[i % 2])(halves[i]))

    def whole(arrays):
        return [(i, i, 0, v.shape[0]) for i, v in enumerate(arrays)]

    early = list(near_lists) + next_lists
    states = {3: attend(asked[3], early, whole(early), None, False, [halves[0]], "attend_early_3")}
    (query_copy,) = join([queries], [[(0, 0, rows)]], [states[3][1], asked[2]], "hold_queries")
    asked[1] = across_z(1)(query_copy)
    states[2] = attend(asked[2], early, whole(early), None, False, [query_copy], "attend_early_2")
    returned, after = [], [states[2][1]]
    for bits in (3, 2):
        (part,) = attend(
            asked[bits], far_lists, whole(far_lists), states[bits], True, after, f"attend_far_{bits}"
        )
        after = [part]
        returned.append(across_z(bits)(part))
    every = early + far_lists
    (part,) = attend(asked[1], every, whole(every), None, True, after, "attend_all_1")
    returned.append(across_z(1)(part))
    rest = next_lists + far_lists
    own = attend(queries, rest, whole(rest), own, False, [part], "attend_own_rest")
    mine, near, far = combine(own, returned)
    far = across_head(2)(far)
    attended = place(h, mine, across_head(1)(near), far, across_head(1)(far[piece:]))
    return (attended, fresh_keys, fresh_values)


def solution(mesh):
    placed = (
        P(("patch", "head"), None),
        P(),
        P(),
        P(None, "head"),
        P(None, "head"),
        P(None, "head"),
        P(),
        P(),
        P("patch", "head"),
        P("patch", "head"),
        P(None, "head"),
        P(None, "head"),
    )
    return jax.shard_map(
        local,
        mesh=mesh,
        in_specs=placed,
        out_specs=(P(("patch", "head"), None), P("patch", "head"), P("patch", "head")),
        check_vma=False,
    )
```

```python
import functools
import math

import jax
import jax.numpy as jnp
from jax import lax
from jax.experimental import pallas as pl
from jax.experimental.pallas import tpu as pltpu
from jax.sharding import PartitionSpec as P

SIDE = 128
THETA = 10000.0
EPS = 1e-06
HS = 128
LOG2E = math.log2(math.e)
VMEM = pl.BlockSpec(memory_space=pltpu.VMEM)
SMEM = pl.BlockSpec(memory_space=pltpu.SMEM)
ANY = pl.BlockSpec(memory_space=pl.ANY)
HBM = pl.BlockSpec(memory_space=pltpu.HBM)
PACK = 4 * 2**20
PROJECT = 20 * 2**20


def patch_permute(move):
    pairs = []
    for y in range(4):
        for x in range(4):
            for z in range(4):
                ty, tx, tz = move(y, x, z)
                pairs.append(((y * 4 + x) * 4 + z, (ty * 4 + tx) * 4 + tz))
    return lambda v: lax.ppermute(v, "patch", pairs)


def along_x(d):
    return patch_permute(lambda y, x, z: (y, (x + d) % 4, z))


def along_y(d):
    return patch_permute(lambda y, x, z: ((y + d) % 4, x, z))


def across_z(bits):
    return patch_permute(lambda y, x, z: (y, x, z ^ bits))


def across_head(bits):
    return lambda v: lax.ppermute(v, "head", [(h, h ^ bits) for h in range(4)])


def rotary(positions):
    half = HS // 2
    first = half // 8
    row_count = (half - first) // 2
    col_count = half - first - row_count
    index = jnp.arange(half).astype(jnp.float32)
    grid_row = (positions // SIDE).astype(jnp.float32)[:, None]
    grid_col = (positions % SIDE).astype(jnp.float32)[:, None]
    row_freq = jnp.power(THETA, -(index - first) / row_count)
    col_freq = jnp.power(THETA, -(index - first - row_count) / col_count)
    angle = jnp.where(
        index < first,
        0.0 * grid_row,
        jnp.where(index < first + row_count, grid_row * row_freq, grid_col * col_freq),
    )
    cosine, sine = jnp.cos(angle), jnp.sin(angle)
    return jnp.concatenate([cosine, cosine], 1), jnp.concatenate([-sine, sine], 1)


def project_kernel(
    h_ref, a0, a1, a2, a3, shift, scale, wq, wk, wv, qg, kg, cos, sin, q_out, k_out, v_out, mod
):
    for j, a in enumerate((a0, a1, a2, a3)):
        values = a[...].astype(jnp.float32)
        centred = values - jnp.mean(values, -1, keepdims=True)
        variance = jnp.mean(centred * centred, -1, keepdims=True)
        normed = centred * lax.rsqrt(variance + EPS)
        mod[j * 64 : j * 64 + 64, :] = (normed * (1.0 + scale[...]) + shift[...]).astype(jnp.bfloat16)

    def norm_rotate(full, gain, store):
        for n in range(full.shape[1] // HS):
            u = full[:, n * HS : n * HS + HS]
            squares = jnp.mean(u * u, -1, keepdims=True)
            u = u * lax.rsqrt(squares + EPS) * gain[...]
            turned = u * cos[...] + pltpu.roll(u, HS // 2, 1) * sin[...]
            store(n, turned.astype(jnp.bfloat16))

    h = h_ref[0]

    def ordered(out, n, block):
        for j in range(4):
            row = pl.multiple_of((h ^ j) * 64, 64)
            out[pl.ds(row, 64), n * HS : n * HS + HS] = block[j * 64 : j * 64 + 64]

    def store_q(n, block):
        q_out[:, n * HS : n * HS + HS] = block

    norm_rotate(jnp.dot(mod[...], wq[...], preferred_element_type=jnp.float32), qg, store_q)
    norm_rotate(
        jnp.dot(mod[...], wk[...], preferred_element_type=jnp.float32), kg, functools.partial(ordered, k_out)
    )
    values = jnp.dot(mod[...], wv[...], preferred_element_type=jnp.float32).astype(jnp.bfloat16)
    for n in range(values.shape[1] // HS):
        ordered(v_out, n, values[:, n * HS : n * HS + HS])


def project(h, pieces, shift, scale, wq, wk, wv, qg, kg, cos, sin):
    rows, width = 4 * pieces[0].shape[0], wq.shape[1]
    out = jax.ShapeDtypeStruct((rows, width), jnp.bfloat16)
    return pl.pallas_call(
        project_kernel,
        out_shape=[out] * 3,
        in_specs=[SMEM] + [VMEM] * 13,
        out_specs=[VMEM] * 3,
        scratch_shapes=[
            pltpu.VMEM((rows, wq.shape[0]), jnp.bfloat16),
        ],
        compiler_params=pltpu.CompilerParams(vmem_limit_bytes=PROJECT),
        name="project",
    )(h, *pieces, shift[None], scale[None], wq, wk, wv, qg[None], kg[None], cos, sin)


def pack_kernel(k, v, after, a, b, sems):
    half, width = a.shape[0], k.shape[1]
    copies = []
    for i, out in enumerate((a, b)):
        for j, source in enumerate((k, v)):
            copies.append(
                pltpu.make_async_copy(
                    source.at[i * half : i * half + half],
                    out.at[:, j * width : j * width + width],
                    sems.at[2 * i + j],
                )
            )
    for c in copies:
        c.start()
    for c in copies:
        c.wait()


def pack(k, v, after):
    out = jax.ShapeDtypeStruct((k.shape[0] // 2, 2 * k.shape[1]), k.dtype)
    return pl.pallas_call(
        pack_kernel,
        out_shape=[out, out],
        in_specs=[HBM] * 2 + [ANY],
        out_specs=[VMEM] * 2,
        scratch_shapes=[pltpu.SemaphoreType.DMA((4,))],
        compiler_params=pltpu.CompilerParams(vmem_limit_bytes=PACK),
        cost_estimate=pl.CostEstimate(flops=0, bytes_accessed=4 * 2**20, transcendentals=0),
        name="pack",
    )(k, v, after)


def join_kernel(*refs, groups, count):
    sources, outs = refs[:count], refs[-len(groups) :]
    for out, group in zip(outs, groups):
        at = 0
        for i, start, size in group:
            out[at : at + size] = sources[i][start : start + size]
            at += size


def join(sources, groups, after, name):
    return pl.pallas_call(
        functools.partial(join_kernel, groups=groups, count=len(sources)),
        out_shape=[
            jax.ShapeDtypeStruct((sum(g[2] for g in group), sources[group[0][0]].shape[1]), jnp.bfloat16)
            for group in groups
        ],
        in_specs=[VMEM] * len(sources) + [ANY] * len(after),
        out_specs=[VMEM] * len(groups),
        compiler_params=pltpu.CompilerParams(vmem_limit_bytes=8 * 2**20),
        cost_estimate=pl.CostEstimate(flops=0, bytes_accessed=2 * 2**20, transcendentals=0),
        name=name,
    )(*sources, *after)


def touch_kernel(*refs):
    refs[-1][...] = jnp.zeros_like(refs[-1])


def touch(arrays, after):
    return pl.pallas_call(
        touch_kernel,
        out_shape=jax.ShapeDtypeStruct((16, HS), jnp.bfloat16),
        in_specs=[VMEM] * len(arrays) + [ANY] * len(after),
        out_specs=VMEM,
        compiler_params=pltpu.CompilerParams(vmem_limit_bytes=2**20),
        name="touch",
    )(*arrays, *after)


def attend_kernel(q_ref, *refs, tiles, count, resumed, last, outputs):
    sources, outs = refs[:count], refs[-outputs:]
    factor = LOG2E / math.sqrt(HS)
    rows, width = q_ref.shape
    half = rows // 2
    heads = width // HS
    lane = lax.broadcasted_iota(jnp.int32, (rows, HS), 1)
    lanes = jnp.zeros((rows, HS), jnp.float32)

    def load(parts):
        return jnp.concatenate([sources[i][start : start + size, c : c + HS] for i, start, size, c in parts], 0)

    for n in range(heads):
        cols = slice(n * HS, n * HS + HS)
        q = q_ref[:, cols]
        top = acc = None
        if resumed:
            sums, tops = refs[count], refs[count + 1]
            top = tops[:, n : n + 1]
            total = jnp.broadcast_to(tops[:, 4 + n : 5 + n], (rows, HS))
            acc = jnp.concatenate([sums[:, cols], total], 1)
        for tile in tiles:
            k = load([(ki, start, size, n * HS) for ki, vi, start, size in tile])
            v = load([(vi, start, size, n * HS + (width if vi == ki else 0)) for ki, vi, start, size in tile])
            s = lax.dot_general(q, k, (((1,), (1,)), ((), ())), preferred_element_type=jnp.float32)
            new = jnp.max(s, -1, keepdims=True)
            if top is not None:
                new = jnp.maximum(top, new)
            p = jnp.exp2((s - new) * factor).astype(jnp.bfloat16)
            part = jnp.dot(p, jnp.concatenate([v, jnp.ones_like(v)], 1), preferred_element_type=jnp.float32)
            acc = part if top is None else acc * jnp.exp2((top - new) * factor) + part
            top = new
        total = acc[:, HS : HS + 1]
        if not last:
            outs[0][:, cols] = acc[:, :HS]
            lanes = jnp.where(lane == n, top, jnp.where(lane == 4 + n, total, lanes))
        else:
            done = (acc[:, :HS] / total).astype(jnp.bfloat16)
            outs[0][:half, cols] = done[half:]
            if outputs == 2:
                outs[1][:, cols] = done[:half]
            else:
                outs[0][half + 16 :, cols] = done[:half]
            log = top * factor + jnp.log2(total)
            for t in range(3):
                term = log.astype(jnp.bfloat16).astype(jnp.float32)
                lanes = jnp.where(lane == 4 * t + n, term, lanes)
                log = log - term
    if not last:
        outs[1][...] = lanes
    else:
        outs[0][half : half + 16, :rows] = lanes.T[:16].astype(jnp.bfloat16)
        outs[0][half : half + 16, rows:] = jnp.zeros((16, width - rows), jnp.bfloat16)


def attend(q, sources, segments, state, last, after, name, whole=False):
    rows, width = q.shape
    tiles, span = [[]], 0
    for segment in segments:
        if sum(t[3] for t in tiles[-1]) + segment[3] > 1152:
            tiles.append([])
        tiles[-1].append(segment)
        span += segment[3]
    if last:
        out_shape = [
            jax.ShapeDtypeStruct((rows // 2 + 16, width), jnp.bfloat16),
            jax.ShapeDtypeStruct((rows // 2, width), jnp.bfloat16),
        ]
        if whole:
            out_shape = [jax.ShapeDtypeStruct((rows + 16, width), jnp.bfloat16)]
    else:
        out_shape = [
            jax.ShapeDtypeStruct((rows, width), jnp.float32),
            jax.ShapeDtypeStruct((rows, HS), jnp.float32),
        ]
    state = list(state or ())
    return pl.pallas_call(
        functools.partial(
            attend_kernel, tiles=tiles, count=len(sources), resumed=bool(state), last=last, outputs=len(out_shape)
        ),
        out_shape=out_shape,
        in_specs=[VMEM] * (1 + len(sources) + len(state)) + [ANY] * len(after),
        out_specs=[VMEM] * len(out_shape),
        compiler_params=pltpu.CompilerParams(vmem_limit_bytes=16 * 2**20),
        cost_estimate=pl.CostEstimate(
            flops=8 * rows * width * span, bytes_accessed=4 * span * width, transcendentals=rows * span * 3
        ),
        name=name,
    )(q, *sources, *state, *after)


def combine_kernel(own, tops, *refs, start, size, count):
    sources, outs = refs[:count], refs[count:]
    rows, width = own.shape
    factor = LOG2E / math.sqrt(HS)
    heads = width // HS
    state = tops[...].T
    totals = state[4:8]
    first = lax.broadcasted_iota(jnp.int32, totals.shape, 0) < heads
    totals = jnp.where(first, totals, 1.0)
    logs = [state[:4] * factor + jnp.log2(totals)]
    for o in sources[:3]:
        terms = o[size : size + 16, :rows].astype(jnp.float32)
        logs.append(terms[:4] + terms[4:8] + terms[8:12])
    top = functools.reduce(jnp.maximum, logs)
    weights = [jnp.exp2(l - top) for l in logs]
    total = functools.reduce(jnp.add, weights)
    pad = jnp.zeros((HS - 4, size), jnp.float32)
    weights = [w / total for w in weights]
    weights[0] = weights[0] / totals
    weights = [jnp.concatenate([w[:, start : start + size], pad], 0).T for w in weights]
    for n in range(heads):
        cols = slice(n * HS, n * HS + HS)
        values = [own[start : start + size, cols]]
        values += [o[:size, cols].astype(jnp.float32) for o in sources[-3:-1]]
        rest = sources[-1]
        values.append((rest[:size, cols] if start else rest[size + 16 :, cols]).astype(jnp.float32))
        out = functools.reduce(jnp.add, [w[:, n : n + 1] * v for w, v in zip(weights, values)])
        out = out.astype(jnp.bfloat16)
        each = size // len(outs)
        for i, ref in enumerate(outs):
            ref[:, cols] = out[i * each : i * each + each]


def combine(own, others, start, size, pieces, name):
    width = own[0].shape[1]
    piece = jax.ShapeDtypeStruct((size // pieces, width), jnp.bfloat16)
    return pl.pallas_call(
        functools.partial(combine_kernel, start=start, size=size, count=len(others)),
        out_shape=[piece] * pieces,
        in_specs=[VMEM] * (2 + len(others)),
        out_specs=[VMEM] * pieces,
        compiler_params=pltpu.CompilerParams(vmem_limit_bytes=8 * 2**20),
        name=name,
    )(*own, *others)


def place_kernel(h_ref, mine, near, far, far_near, out):
    width = near.shape[1]
    h = h_ref[0]
    pieces = (mine[...], near[...], far[:64], far_near[...])
    for j, piece in enumerate(pieces):
        out[:, pl.ds(pl.multiple_of((h ^ j) * width, HS), width)] = piece


def place(h, mine, near, far, far_near):
    return pl.pallas_call(
        place_kernel,
        out_shape=jax.ShapeDtypeStruct((64, 4 * near.shape[1]), jnp.bfloat16),
        in_specs=[SMEM] + [VMEM] * 4,
        out_specs=VMEM,
        compiler_params=pltpu.CompilerParams(vmem_limit_bytes=4 * 2**20),
        name="place",
    )(h, mine, near, far, far_near)


def local(
    image_tokens,
    shift,
    scale,
    w_query,
    w_key,
    w_value,
    q_gain,
    k_gain,
    stale_keys,
    stale_values,
    text_keys,
    text_values,
):
    rows = stale_keys.shape[0]
    piece = image_tokens.shape[0]
    head = lax.axis_index("head").astype(jnp.int32)
    h = head[None]
    order = (head ^ jnp.arange(4, dtype=jnp.int32))[:, None] * piece + jnp.arange(piece, dtype=jnp.int32)
    cos, sin = rotary(lax.axis_index("patch") * rows + order.reshape(-1))

    far_rows = across_head(2)(image_tokens)
    beside_rows = across_head(1)(image_tokens)
    pieces = [image_tokens, beside_rows, far_rows, across_head(1)(far_rows)]

    half = rows // 2
    packed = pack(stale_keys, stale_values, beside_rows)
    ways = (along_x, along_y)
    beside = [along(d)(v) for v, along in zip(packed, ways) for d in (1, 3)]
    again = join(packed, [[(0, 0, half)], [(1, 0, half)]], beside[:2], "hold_first")
    across = [along(2)(v) for v, along in zip(again, ways)]
    touched = touch([w_key, w_value], [again[0], cos, sin])
    near_lists = join(
        [packed[0], *beside[:2], across[0], packed[1], *beside[2:], across[1]],
        [[(4 * g + i, 0, half) for i in range(4)] for g in range(2)],
        [touched],
        "join_lines",
    )
    next_lists = []
    for v, along in zip(near_lists, (along_y, along_x)):
        next_lists += [along(1)(v), along(3)(v)]

    queries, fresh_keys, fresh_values = project(
        h, pieces, shift, scale, w_query, w_key, w_value, q_gain, k_gain, cos, sin
    )
    asked = {3: across_z(3)(queries), 2: across_z(2)(queries)}

    text = text_keys.shape[0]
    own = attend(
        queries,
        list(near_lists) + [text_keys, text_values, fresh_keys, fresh_values],
        [(2, 3, 0, text), (4, 5, 0, rows), (0, 0, half, 3 * half), (1, 1, half, 3 * half)],
        None,
        False,
        [],
        "attend_own_near",
    )
    halves = join(
        next_lists, [[(i, (i % 2) * 2 * half, 2 * half)] for i in range(4)], [own[1]], "join_halves"
    )
    far_lists = []
    for i, along in enumerate((along_y, along_y, along_x, along_x)):
        far_lists.append(along((1, 3)[i % 2])(halves[i]))

    def whole(arrays):
        return [(i, i, 0, v.shape[0]) for i, v in enumerate(arrays)]

    early = list(near_lists) + next_lists
    states = {3: attend(asked[3], early, whole(early), None, False, [halves[0]], "attend_early_3")}
    (query_copy,) = join([queries], [[(0, 0, rows)]], [states[3][1], asked[2]], "hold_queries")
    asked[1] = across_z(1)(query_copy)
    states[2] = attend(asked[2], early, whole(early), None, False, [query_copy], "attend_early_2")
    back, kept, after = [], [], [states[2][1]]
    for bits in (3, 2):
        part, rest = attend(
            asked[bits], far_lists, whole(far_lists), states[bits], True, after, f"attend_far_{bits}"
        )
        after = [part]
        back.append(across_z(bits)(part))
        kept.append(rest)
    every = early + far_lists
    (part,) = attend(asked[1], every, whole(every), None, True, after, "attend_all_1", True)
    back.append(across_z(1)(part))
    kept = join(kept, [[(i, 0, half)] for i in range(2)], [part], "hold_near_rows")
    rest = next_lists + far_lists
    own = attend(queries, rest, whole(rest), own, False, [kept[0]], "attend_own_rest")
    kept = [across_z(bits)(v) for bits, v in zip((3, 2), kept)]
    (far,) = combine(own, back, half, half, 1, "combine_far")
    far = across_head(2)(far)
    mine, near = combine(own, back[:2] + [back[2]] + kept + [back[2]], 0, half, 2, "combine_near")
    attended = place(h, mine, across_head(1)(near), far, across_head(1)(far[piece:]))
    return (attended, fresh_keys, fresh_values)


def solution(mesh):
    placed = (
        P(("patch", "head"), None),
        P(),
        P(),
        P(None, "head"),
        P(None, "head"),
        P(None, "head"),
        P(),
        P(),
        P("patch", "head"),
        P("patch", "head"),
        P(None, "head"),
        P(None, "head"),
    )
    return jax.shard_map(
        local,
        mesh=mesh,
        in_specs=placed,
        out_specs=(P(("patch", "head"), None), P("patch", "head"), P("patch", "head")),
        check_vma=False,
    )
```

```python
import functools
import math

import jax
import jax.numpy as jnp
from jax import lax
from jax.experimental import pallas as pl
from jax.experimental.pallas import tpu as pltpu
from jax.sharding import PartitionSpec as P

SIDE = 128
THETA = 10000.0
EPS = 1e-06
HS = 128
LOG2E = math.log2(math.e)
VMEM = pl.BlockSpec(memory_space=pltpu.VMEM)
SMEM = pl.BlockSpec(memory_space=pltpu.SMEM)
ANY = pl.BlockSpec(memory_space=pl.ANY)
HBM = pl.BlockSpec(memory_space=pltpu.HBM)
PACK = 4 * 2**20
PROJECT = 20 * 2**20


def patch_permute(move):
    pairs = []
    for y in range(4):
        for x in range(4):
            for z in range(4):
                ty, tx, tz = move(y, x, z)
                pairs.append(((y * 4 + x) * 4 + z, (ty * 4 + tx) * 4 + tz))
    return lambda v: lax.ppermute(v, "patch", pairs)


def along_x(d):
    return patch_permute(lambda y, x, z: (y, (x + d) % 4, z))


def along_y(d):
    return patch_permute(lambda y, x, z: ((y + d) % 4, x, z))


def across_z(bits):
    return patch_permute(lambda y, x, z: (y, x, z ^ bits))


def across_head(bits):
    return lambda v: lax.ppermute(v, "head", [(h, h ^ bits) for h in range(4)])


def rotary(positions):
    half = HS // 2
    first = half // 8
    row_count = (half - first) // 2
    col_count = half - first - row_count
    index = jnp.arange(half).astype(jnp.float32)
    grid_row = (positions // SIDE).astype(jnp.float32)[:, None]
    grid_col = (positions % SIDE).astype(jnp.float32)[:, None]
    row_freq = jnp.power(THETA, -(index - first) / row_count)
    col_freq = jnp.power(THETA, -(index - first - row_count) / col_count)
    angle = jnp.where(
        index < first,
        0.0 * grid_row,
        jnp.where(index < first + row_count, grid_row * row_freq, grid_col * col_freq),
    )
    cosine, sine = jnp.cos(angle), jnp.sin(angle)
    return jnp.concatenate([cosine, cosine], 1), jnp.concatenate([-sine, sine], 1)


def project_kernel(
    h_ref, a0, a1, a2, a3, shift, scale, wq, wk, wv, qg, kg, cos, sin, q_out, k_out, v_out, mod
):
    for j, a in enumerate((a0, a1, a2, a3)):
        values = a[...].astype(jnp.float32)
        centred = values - jnp.mean(values, -1, keepdims=True)
        variance = jnp.mean(centred * centred, -1, keepdims=True)
        normed = centred * lax.rsqrt(variance + EPS)
        mod[j * 64 : j * 64 + 64, :] = (normed * (1.0 + scale[...]) + shift[...]).astype(jnp.bfloat16)

    def norm_rotate(full, gain, store):
        for n in range(full.shape[1] // HS):
            u = full[:, n * HS : n * HS + HS]
            squares = jnp.mean(u * u, -1, keepdims=True)
            u = u * lax.rsqrt(squares + EPS) * gain[...]
            turned = u * cos[...] + pltpu.roll(u, HS // 2, 1) * sin[...]
            store(n, turned.astype(jnp.bfloat16))

    h = h_ref[0]

    def ordered(out, n, block):
        for j in range(4):
            row = pl.multiple_of((h ^ j) * 64, 64)
            out[pl.ds(row, 64), n * HS : n * HS + HS] = block[j * 64 : j * 64 + 64]

    def store_q(n, block):
        q_out[:, n * HS : n * HS + HS] = block

    norm_rotate(jnp.dot(mod[...], wq[...], preferred_element_type=jnp.float32), qg, store_q)
    norm_rotate(
        jnp.dot(mod[...], wk[...], preferred_element_type=jnp.float32), kg, functools.partial(ordered, k_out)
    )
    values = jnp.dot(mod[...], wv[...], preferred_element_type=jnp.float32).astype(jnp.bfloat16)
    for n in range(values.shape[1] // HS):
        ordered(v_out, n, values[:, n * HS : n * HS + HS])


def project(h, pieces, shift, scale, wq, wk, wv, qg, kg, cos, sin):
    rows, width = 4 * pieces[0].shape[0], wq.shape[1]
    out = jax.ShapeDtypeStruct((rows, width), jnp.bfloat16)
    return pl.pallas_call(
        project_kernel,
        out_shape=[out] * 3,
        in_specs=[SMEM] + [VMEM] * 13,
        out_specs=[VMEM] * 3,
        scratch_shapes=[
            pltpu.VMEM((rows, wq.shape[0]), jnp.bfloat16),
        ],
        compiler_params=pltpu.CompilerParams(vmem_limit_bytes=PROJECT),
        name="project",
    )(h, *pieces, shift[None], scale[None], wq, wk, wv, qg[None], kg[None], cos, sin)


def pack_kernel(k, v, after, a, b, sems):
    half, width = a.shape[0], k.shape[1]
    copies = []
    for i, out in enumerate((a, b)):
        for j, source in enumerate((k, v)):
            copies.append(
                pltpu.make_async_copy(
                    source.at[i * half : i * half + half],
                    out.at[:, j * width : j * width + width],
                    sems.at[2 * i + j],
                )
            )
    for c in copies:
        c.start()
    for c in copies:
        c.wait()


def pack(k, v, after):
    out = jax.ShapeDtypeStruct((k.shape[0] // 2, 2 * k.shape[1]), k.dtype)
    return pl.pallas_call(
        pack_kernel,
        out_shape=[out, out],
        in_specs=[HBM] * 2 + [ANY],
        out_specs=[VMEM] * 2,
        scratch_shapes=[pltpu.SemaphoreType.DMA((4,))],
        compiler_params=pltpu.CompilerParams(vmem_limit_bytes=PACK),
        cost_estimate=pl.CostEstimate(flops=0, bytes_accessed=4 * 2**20, transcendentals=0),
        name="pack",
    )(k, v, after)


def join_kernel(*refs, groups, count):
    sources, outs = refs[:count], refs[-len(groups) :]
    for out, group in zip(outs, groups):
        at = 0
        for i, start, size in group:
            out[at : at + size] = sources[i][start : start + size]
            at += size


def join(sources, groups, after, name):
    return pl.pallas_call(
        functools.partial(join_kernel, groups=groups, count=len(sources)),
        out_shape=[
            jax.ShapeDtypeStruct((sum(g[2] for g in group), sources[group[0][0]].shape[1]), jnp.bfloat16)
            for group in groups
        ],
        in_specs=[VMEM] * len(sources) + [ANY] * len(after),
        out_specs=[VMEM] * len(groups),
        compiler_params=pltpu.CompilerParams(vmem_limit_bytes=8 * 2**20),
        cost_estimate=pl.CostEstimate(flops=0, bytes_accessed=2 * 2**20, transcendentals=0),
        name=name,
    )(*sources, *after)


def touch_kernel(*refs):
    refs[-1][...] = jnp.zeros_like(refs[-1])


def touch(arrays, after):
    return pl.pallas_call(
        touch_kernel,
        out_shape=jax.ShapeDtypeStruct((16, HS), jnp.bfloat16),
        in_specs=[VMEM] * len(arrays) + [ANY] * len(after),
        out_specs=VMEM,
        compiler_params=pltpu.CompilerParams(vmem_limit_bytes=2**20),
        name="touch",
    )(*arrays, *after)


def attend_kernel(q_ref, *refs, tiles, count, resumed, last, outputs):
    sources, outs = refs[:count], refs[-outputs:]
    factor = LOG2E / math.sqrt(HS)
    rows, width = q_ref.shape
    half = rows // 2
    heads = width // HS
    lane = lax.broadcasted_iota(jnp.int32, (rows, HS), 1)
    lanes = jnp.zeros((rows, HS), jnp.float32)

    def load(parts):
        return jnp.concatenate([sources[i][start : start + size, c : c + HS] for i, start, size, c in parts], 0)

    for n in range(heads):
        cols = slice(n * HS, n * HS + HS)
        q = q_ref[:, cols]
        top = acc = None
        if resumed:
            sums, tops = refs[count], refs[count + 1]
            top = tops[:, n : n + 1]
            total = jnp.broadcast_to(tops[:, 4 + n : 5 + n], (rows, HS))
            acc = jnp.concatenate([sums[:, cols], total], 1)
        for tile in tiles:
            k = load([(ki, start, size, n * HS) for ki, vi, start, size in tile])
            v = load([(vi, start, size, n * HS + (width if vi == ki else 0)) for ki, vi, start, size in tile])
            s = lax.dot_general(q, k, (((1,), (1,)), ((), ())), preferred_element_type=jnp.float32)
            new = jnp.max(s, -1, keepdims=True)
            if top is not None:
                new = jnp.maximum(top, new)
            p = jnp.exp2((s - new) * factor).astype(jnp.bfloat16)
            part = jnp.dot(p, jnp.concatenate([v, jnp.ones_like(v)], 1), preferred_element_type=jnp.float32)
            acc = part if top is None else acc * jnp.exp2((top - new) * factor) + part
            top = new
        total = acc[:, HS : HS + 1]
        if not last:
            outs[0][:, cols] = acc[:, :HS]
            lanes = jnp.where(lane == n, top, jnp.where(lane == 4 + n, total, lanes))
        else:
            done = (acc[:, :HS] / total).astype(jnp.bfloat16)
            outs[0][:half, cols] = done[half:]
            if outputs == 2:
                outs[1][:, cols] = done[:half]
            else:
                outs[0][half + 16 :, cols] = done[:half]
            log = top * factor + jnp.log2(total)
            for t in range(3):
                term = log.astype(jnp.bfloat16).astype(jnp.float32)
                lanes = jnp.where(lane == 4 * t + n, term, lanes)
                log = log - term
    if not last:
        outs[1][...] = lanes
    else:
        outs[0][half : half + 16, :rows] = lanes.T[:16].astype(jnp.bfloat16)
        outs[0][half : half + 16, rows:] = jnp.zeros((16, width - rows), jnp.bfloat16)


def attend(q, sources, segments, state, last, after, name, whole=False):
    rows, width = q.shape
    tiles, span = [[]], 0
    for segment in segments:
        if sum(t[3] for t in tiles[-1]) + segment[3] > 1152:
            tiles.append([])
        tiles[-1].append(segment)
        span += segment[3]
    if last:
        out_shape = [
            jax.ShapeDtypeStruct((rows // 2 + 16, width), jnp.bfloat16),
            jax.ShapeDtypeStruct((rows // 2, width), jnp.bfloat16),
        ]
        if whole:
            out_shape = [jax.ShapeDtypeStruct((rows + 16, width), jnp.bfloat16)]
    else:
        out_shape = [
            jax.ShapeDtypeStruct((rows, width), jnp.float32),
            jax.ShapeDtypeStruct((rows, HS), jnp.float32),
        ]
    state = list(state or ())
    return pl.pallas_call(
        functools.partial(
            attend_kernel, tiles=tiles, count=len(sources), resumed=bool(state), last=last, outputs=len(out_shape)
        ),
        out_shape=out_shape,
        in_specs=[VMEM] * (1 + len(sources) + len(state)) + [ANY] * len(after),
        out_specs=[VMEM] * len(out_shape),
        compiler_params=pltpu.CompilerParams(vmem_limit_bytes=16 * 2**20),
        cost_estimate=pl.CostEstimate(
            flops=8 * rows * width * span, bytes_accessed=4 * span * width, transcendentals=rows * span * 3
        ),
        name=name,
    )(q, *sources, *state, *after)


def combine_kernel(own, tops, *refs, start, size, count):
    sources, outs = refs[:count], refs[count:]
    rows, width = own.shape
    factor = LOG2E / math.sqrt(HS)
    heads = width // HS
    state = tops[...].T
    totals = state[4:8]
    first = lax.broadcasted_iota(jnp.int32, totals.shape, 0) < heads
    totals = jnp.where(first, totals, 1.0)
    logs = [state[:4] * factor + jnp.log2(totals)]
    for o in sources[:3]:
        terms = o[size : size + 16, :rows].astype(jnp.float32)
        logs.append(terms[:4] + terms[4:8] + terms[8:12])
    top = functools.reduce(jnp.maximum, logs)
    weights = [jnp.exp2(l - top) for l in logs]
    total = functools.reduce(jnp.add, weights)
    pad = jnp.zeros((HS - 4, size), jnp.float32)
    weights = [w / total for w in weights]
    weights[0] = weights[0] / totals
    weights = [jnp.concatenate([w[:, start : start + size], pad], 0).T for w in weights]
    for n in range(heads):
        cols = slice(n * HS, n * HS + HS)
        values = [own[start : start + size, cols]]
        values += [o[:size, cols].astype(jnp.float32) for o in sources[-3:-1]]
        rest = sources[-1]
        values.append((rest[:size, cols] if start else rest[size + 16 :, cols]).astype(jnp.float32))
        out = functools.reduce(jnp.add, [w[:, n : n + 1] * v for w, v in zip(weights, values)])
        out = out.astype(jnp.bfloat16)
        each = size // len(outs)
        for i, ref in enumerate(outs):
            ref[:, cols] = out[i * each : i * each + each]


def combine(own, others, start, size, pieces, name):
    width = own[0].shape[1]
    piece = jax.ShapeDtypeStruct((size // pieces, width), jnp.bfloat16)
    return pl.pallas_call(
        functools.partial(combine_kernel, start=start, size=size, count=len(others)),
        out_shape=[piece] * pieces,
        in_specs=[VMEM] * (2 + len(others)),
        out_specs=[VMEM] * pieces,
        compiler_params=pltpu.CompilerParams(vmem_limit_bytes=8 * 2**20),
        name=name,
    )(*own, *others)


def place_kernel(h_ref, mine, near, far, far_near, out):
    width = near.shape[1]
    h = h_ref[0]
    pieces = (mine[...], near[...], far[:64], far_near[...])
    for j, piece in enumerate(pieces):
        out[:, pl.ds(pl.multiple_of((h ^ j) * width, HS), width)] = piece


def place(h, mine, near, far, far_near):
    return pl.pallas_call(
        place_kernel,
        out_shape=jax.ShapeDtypeStruct((64, 4 * near.shape[1]), jnp.bfloat16),
        in_specs=[SMEM] + [VMEM] * 4,
        out_specs=VMEM,
        compiler_params=pltpu.CompilerParams(vmem_limit_bytes=4 * 2**20),
        name="place",
    )(h, mine, near, far, far_near)


def local(
    image_tokens,
    shift,
    scale,
    w_query,
    w_key,
    w_value,
    q_gain,
    k_gain,
    stale_keys,
    stale_values,
    text_keys,
    text_values,
):
    rows = stale_keys.shape[0]
    piece = image_tokens.shape[0]
    head = lax.axis_index("head").astype(jnp.int32)
    h = head[None]
    order = (head ^ jnp.arange(4, dtype=jnp.int32))[:, None] * piece + jnp.arange(piece, dtype=jnp.int32)
    cos, sin = rotary(lax.axis_index("patch") * rows + order.reshape(-1))

    far_rows = across_head(2)(image_tokens)
    beside_rows = across_head(1)(image_tokens)
    pieces = [image_tokens, beside_rows, far_rows, across_head(1)(far_rows)]

    half = rows // 2
    packed = pack(stale_keys, stale_values, beside_rows)
    ways = (along_x, along_y)
    beside = [along(d)(v) for v, along in zip(packed, ways) for d in (1, 3)]
    across = [along(1)(v) for v, along in zip((beside[0], beside[2]), ways)]
    touched = touch([w_key, w_value], [beside[0]])
    near_lists = join(
        [packed[0], *beside[:2], across[0], packed[1], *beside[2:], across[1]],
        [[(4 * g + i, 0, half) for i in range(4)] for g in range(2)],
        [touched],
        "join_lines",
    )
    next_lists = []
    for v, along in zip(near_lists, (along_y, along_x)):
        next_lists += [along(1)(v), along(3)(v)]

    queries, fresh_keys, fresh_values = project(
        h, pieces, shift, scale, w_query, w_key, w_value, q_gain, k_gain, cos, sin
    )
    asked = {3: across_z(3)(queries), 2: across_z(2)(queries)}

    text = text_keys.shape[0]
    own = attend(
        queries,
        list(near_lists) + [text_keys, text_values, fresh_keys, fresh_values],
        [(2, 3, 0, text), (4, 5, 0, rows), (0, 0, half, 3 * half), (1, 1, half, 3 * half)],
        None,
        False,
        [],
        "attend_own_near",
    )
    halves = join(
        next_lists, [[(i, (i % 2) * 2 * half, 2 * half)] for i in range(4)], [own[1]], "join_halves"
    )
    far_lists = []
    for i, along in enumerate((along_y, along_y, along_x, along_x)):
        far_lists.append(along((1, 3)[i % 2])(halves[i]))

    def whole(arrays):
        return [(i, i, 0, v.shape[0]) for i, v in enumerate(arrays)]

    early = list(near_lists) + next_lists
    states = {3: attend(asked[3], early, whole(early), None, False, [halves[0]], "attend_early_3")}
    (query_copy,) = join([queries], [[(0, 0, rows)]], [states[3][1], asked[2]], "hold_queries")
    asked[1] = across_z(1)(query_copy)
    states[2] = attend(asked[2], early, whole(early), None, False, [query_copy], "attend_early_2")
    back, kept, after = [], [], [states[2][1]]
    for bits in (3, 2):
        part, rest = attend(
            asked[bits], far_lists, whole(far_lists), states[bits], True, after, f"attend_far_{bits}"
        )
        after = [part]
        back.append(across_z(bits)(part))
        kept.append(rest)
    every = early + far_lists
    (part,) = attend(asked[1], every, whole(every), None, True, after, "attend_all_1", True)
    back.append(across_z(1)(part))
    kept = join(kept, [[(i, 0, half)] for i in range(2)], [part], "hold_near_rows")
    rest = next_lists + far_lists
    own = attend(queries, rest, whole(rest), own, False, [kept[0]], "attend_own_rest")
    kept = [across_z(bits)(v) for bits, v in zip((3, 2), kept)]
    (far,) = combine(own, back, half, half, 1, "combine_far")
    far = across_head(2)(far)
    mine, near = combine(own, back[:2] + [back[2]] + kept + [back[2]], 0, half, 2, "combine_near")
    attended = place(h, mine, across_head(1)(near), far, across_head(1)(far[piece:]))
    return (attended, fresh_keys, fresh_values)


def solution(mesh):
    placed = (
        P(("patch", "head"), None),
        P(),
        P(),
        P(None, "head"),
        P(None, "head"),
        P(None, "head"),
        P(),
        P(),
        P("patch", "head"),
        P("patch", "head"),
        P(None, "head"),
        P(None, "head"),
    )
    return jax.shard_map(
        local,
        mesh=mesh,
        in_specs=placed,
        out_specs=(P(("patch", "head"), None), P("patch", "head"), P("patch", "head")),
        check_vma=False,
    )
```

```python
import functools
import math

import jax
import jax.numpy as jnp
from jax import lax
from jax.experimental import pallas as pl
from jax.experimental.pallas import tpu as pltpu
from jax.sharding import PartitionSpec as P

SIDE = 128
THETA = 10000.0
EPS = 1e-06
HS = 128
LOG2E = math.log2(math.e)
VMEM = pl.BlockSpec(memory_space=pltpu.VMEM)
SMEM = pl.BlockSpec(memory_space=pltpu.SMEM)
ANY = pl.BlockSpec(memory_space=pl.ANY)
HBM = pl.BlockSpec(memory_space=pltpu.HBM)
PACK = 4 * 2**20
PROJECT = 20 * 2**20


def patch_permute(move):
    pairs = []
    for y in range(4):
        for x in range(4):
            for z in range(4):
                ty, tx, tz = move(y, x, z)
                pairs.append(((y * 4 + x) * 4 + z, (ty * 4 + tx) * 4 + tz))
    return lambda v: lax.ppermute(v, "patch", pairs)


def along_x(d):
    return patch_permute(lambda y, x, z: (y, (x + d) % 4, z))


def along_y(d):
    return patch_permute(lambda y, x, z: ((y + d) % 4, x, z))


def across_z(bits):
    return patch_permute(lambda y, x, z: (y, x, z ^ bits))


def across_head(bits):
    return lambda v: lax.ppermute(v, "head", [(h, h ^ bits) for h in range(4)])


def rotary(positions):
    half = HS // 2
    first = half // 8
    row_count = (half - first) // 2
    col_count = half - first - row_count
    index = jnp.arange(half).astype(jnp.float32)
    grid_row = (positions // SIDE).astype(jnp.float32)[:, None]
    grid_col = (positions % SIDE).astype(jnp.float32)[:, None]
    row_freq = jnp.power(THETA, -(index - first) / row_count)
    col_freq = jnp.power(THETA, -(index - first - row_count) / col_count)
    angle = jnp.where(
        index < first,
        0.0 * grid_row,
        jnp.where(index < first + row_count, grid_row * row_freq, grid_col * col_freq),
    )
    cosine, sine = jnp.cos(angle), jnp.sin(angle)
    return jnp.concatenate([cosine, cosine], 1), jnp.concatenate([-sine, sine], 1)


def project_kernel(
    h_ref, a0, a1, a2, a3, shift, scale, wq, wk, wv, qg, kg, cos, sin, q_out, k_out, v_out, mod
):
    for j, a in enumerate((a0, a1, a2, a3)):
        values = a[...].astype(jnp.float32)
        centred = values - jnp.mean(values, -1, keepdims=True)
        variance = jnp.mean(centred * centred, -1, keepdims=True)
        normed = centred * lax.rsqrt(variance + EPS)
        mod[j * 64 : j * 64 + 64, :] = (normed * (1.0 + scale[...]) + shift[...]).astype(jnp.bfloat16)

    def norm_rotate(full, gain, store):
        for n in range(full.shape[1] // HS):
            u = full[:, n * HS : n * HS + HS]
            squares = jnp.mean(u * u, -1, keepdims=True)
            u = u * lax.rsqrt(squares + EPS) * gain[...]
            turned = u * cos[...] + pltpu.roll(u, HS // 2, 1) * sin[...]
            store(n, turned.astype(jnp.bfloat16))

    h = h_ref[0]

    def ordered(out, n, block):
        for j in range(4):
            row = pl.multiple_of((h ^ j) * 64, 64)
            out[pl.ds(row, 64), n * HS : n * HS + HS] = block[j * 64 : j * 64 + 64]

    def store_q(n, block):
        q_out[:, n * HS : n * HS + HS] = block

    norm_rotate(jnp.dot(mod[...], wq[...], preferred_element_type=jnp.float32), qg, store_q)
    norm_rotate(
        jnp.dot(mod[...], wk[...], preferred_element_type=jnp.float32), kg, functools.partial(ordered, k_out)
    )
    values = jnp.dot(mod[...], wv[...], preferred_element_type=jnp.float32).astype(jnp.bfloat16)
    for n in range(values.shape[1] // HS):
        ordered(v_out, n, values[:, n * HS : n * HS + HS])


def project(h, pieces, shift, scale, wq, wk, wv, qg, kg, cos, sin):
    rows, width = 4 * pieces[0].shape[0], wq.shape[1]
    out = jax.ShapeDtypeStruct((rows, width), jnp.bfloat16)
    return pl.pallas_call(
        project_kernel,
        out_shape=[out] * 3,
        in_specs=[SMEM] + [VMEM] * 13,
        out_specs=[VMEM] * 3,
        scratch_shapes=[
            pltpu.VMEM((rows, wq.shape[0]), jnp.bfloat16),
        ],
        compiler_params=pltpu.CompilerParams(vmem_limit_bytes=PROJECT),
        name="project",
    )(h, *pieces, shift[None], scale[None], wq, wk, wv, qg[None], kg[None], cos, sin)


def pack_kernel(k, v, after, a, b, sems):
    half, width = a.shape[0], k.shape[1]
    copies = []
    for i, out in enumerate((a, b)):
        for j, source in enumerate((k, v)):
            copies.append(
                pltpu.make_async_copy(
                    source.at[i * half : i * half + half],
                    out.at[:, j * width : j * width + width],
                    sems.at[2 * i + j],
                )
            )
    for c in copies:
        c.start()
    for c in copies:
        c.wait()


def pack(k, v, after):
    out = jax.ShapeDtypeStruct((k.shape[0] // 2, 2 * k.shape[1]), k.dtype)
    return pl.pallas_call(
        pack_kernel,
        out_shape=[out, out],
        in_specs=[HBM] * 2 + [ANY],
        out_specs=[VMEM] * 2,
        scratch_shapes=[pltpu.SemaphoreType.DMA((4,))],
        compiler_params=pltpu.CompilerParams(vmem_limit_bytes=PACK),
        cost_estimate=pl.CostEstimate(flops=0, bytes_accessed=4 * 2**20, transcendentals=0),
        name="pack",
    )(k, v, after)


def join_kernel(*refs, groups, count):
    sources, outs = refs[:count], refs[-len(groups) :]
    for out, group in zip(outs, groups):
        at = 0
        for i, start, size in group:
            out[at : at + size] = sources[i][start : start + size]
            at += size


def join(sources, groups, after, name):
    return pl.pallas_call(
        functools.partial(join_kernel, groups=groups, count=len(sources)),
        out_shape=[
            jax.ShapeDtypeStruct((sum(g[2] for g in group), sources[group[0][0]].shape[1]), jnp.bfloat16)
            for group in groups
        ],
        in_specs=[VMEM] * len(sources) + [ANY] * len(after),
        out_specs=[VMEM] * len(groups),
        compiler_params=pltpu.CompilerParams(vmem_limit_bytes=8 * 2**20),
        cost_estimate=pl.CostEstimate(flops=0, bytes_accessed=2 * 2**20, transcendentals=0),
        name=name,
    )(*sources, *after)


def touch_kernel(*refs):
    refs[-1][...] = jnp.zeros_like(refs[-1])


def touch(arrays, after):
    return pl.pallas_call(
        touch_kernel,
        out_shape=jax.ShapeDtypeStruct((16, HS), jnp.bfloat16),
        in_specs=[VMEM] * len(arrays) + [ANY] * len(after),
        out_specs=VMEM,
        compiler_params=pltpu.CompilerParams(vmem_limit_bytes=2**20),
        name="touch",
    )(*arrays, *after)


def attend_kernel(q_ref, *refs, tiles, count, resumed, last, outputs):
    sources, outs = refs[:count], refs[-outputs:]
    factor = LOG2E / math.sqrt(HS)
    rows, width = q_ref.shape
    half = rows // 2
    heads = width // HS
    lane = lax.broadcasted_iota(jnp.int32, (rows, HS), 1)
    lanes = jnp.zeros((rows, HS), jnp.float32)

    def load(parts):
        return jnp.concatenate([sources[i][start : start + size, c : c + HS] for i, start, size, c in parts], 0)

    for n in range(heads):
        cols = slice(n * HS, n * HS + HS)
        q = q_ref[:, cols]
        top = acc = None
        if resumed:
            sums, tops = refs[count], refs[count + 1]
            top = tops[:, n : n + 1]
            total = jnp.broadcast_to(tops[:, 4 + n : 5 + n], (rows, HS))
            acc = jnp.concatenate([sums[:, cols], total], 1)
        for tile in tiles:
            k = load([(ki, start, size, n * HS) for ki, vi, start, size in tile])
            v = load([(vi, start, size, n * HS + (width if vi == ki else 0)) for ki, vi, start, size in tile])
            s = lax.dot_general(q, k, (((1,), (1,)), ((), ())), preferred_element_type=jnp.float32)
            new = jnp.max(s, -1, keepdims=True)
            if top is not None:
                new = jnp.maximum(top, new)
            p = jnp.exp2((s - new) * factor).astype(jnp.bfloat16)
            part = jnp.dot(p, jnp.concatenate([v, jnp.ones_like(v)], 1), preferred_element_type=jnp.float32)
            acc = part if top is None else acc * jnp.exp2((top - new) * factor) + part
            top = new
        total = acc[:, HS : HS + 1]
        if not last:
            outs[0][:, cols] = acc[:, :HS]
            lanes = jnp.where(lane == n, top, jnp.where(lane == 4 + n, total, lanes))
        else:
            done = (acc[:, :HS] / total).astype(jnp.bfloat16)
            outs[0][:half, cols] = done[half:]
            if outputs == 2:
                outs[1][:, cols] = done[:half]
            else:
                outs[0][half + 16 :, cols] = done[:half]
            log = top * factor + jnp.log2(total)
            for t in range(3):
                term = log.astype(jnp.bfloat16).astype(jnp.float32)
                lanes = jnp.where(lane == 4 * t + n, term, lanes)
                log = log - term
    if not last:
        outs[1][...] = lanes
    else:
        outs[0][half : half + 16, :rows] = lanes.T[:16].astype(jnp.bfloat16)
        outs[0][half : half + 16, rows:] = jnp.zeros((16, width - rows), jnp.bfloat16)


def attend(q, sources, segments, state, last, after, name, whole=False):
    rows, width = q.shape
    tiles, span = [[]], 0
    for segment in segments:
        if sum(t[3] for t in tiles[-1]) + segment[3] > 1152:
            tiles.append([])
        tiles[-1].append(segment)
        span += segment[3]
    if last:
        out_shape = [
            jax.ShapeDtypeStruct((rows // 2 + 16, width), jnp.bfloat16),
            jax.ShapeDtypeStruct((rows // 2, width), jnp.bfloat16),
        ]
        if whole:
            out_shape = [jax.ShapeDtypeStruct((rows + 16, width), jnp.bfloat16)]
    else:
        out_shape = [
            jax.ShapeDtypeStruct((rows, width), jnp.float32),
            jax.ShapeDtypeStruct((rows, HS), jnp.float32),
        ]
    state = list(state or ())
    return pl.pallas_call(
        functools.partial(
            attend_kernel, tiles=tiles, count=len(sources), resumed=bool(state), last=last, outputs=len(out_shape)
        ),
        out_shape=out_shape,
        in_specs=[VMEM] * (1 + len(sources) + len(state)) + [ANY] * len(after),
        out_specs=[VMEM] * len(out_shape),
        compiler_params=pltpu.CompilerParams(vmem_limit_bytes=16 * 2**20),
        cost_estimate=pl.CostEstimate(
            flops=8 * rows * width * span, bytes_accessed=4 * span * width, transcendentals=rows * span * 3
        ),
        name=name,
    )(q, *sources, *state, *after)


def combine_kernel(own, tops, *refs, start, size, count):
    sources, outs = refs[:count], refs[count:]
    rows, width = own.shape
    factor = LOG2E / math.sqrt(HS)
    heads = width // HS
    state = tops[...].T
    totals = state[4:8]
    first = lax.broadcasted_iota(jnp.int32, totals.shape, 0) < heads
    totals = jnp.where(first, totals, 1.0)
    logs = [state[:4] * factor + jnp.log2(totals)]
    for o in sources[:3]:
        terms = o[size : size + 16, :rows].astype(jnp.float32)
        logs.append(terms[:4] + terms[4:8] + terms[8:12])
    top = functools.reduce(jnp.maximum, logs)
    weights = [jnp.exp2(l - top) for l in logs]
    total = functools.reduce(jnp.add, weights)
    pad = jnp.zeros((HS - 4, size), jnp.float32)
    weights = [w / total for w in weights]
    weights[0] = weights[0] / totals
    weights = [jnp.concatenate([w[:, start : start + size], pad], 0).T for w in weights]
    for n in range(heads):
        cols = slice(n * HS, n * HS + HS)
        values = [own[start : start + size, cols]]
        values += [o[:size, cols].astype(jnp.float32) for o in sources[-3:-1]]
        rest = sources[-1]
        values.append((rest[:size, cols] if start else rest[size + 16 :, cols]).astype(jnp.float32))
        out = functools.reduce(jnp.add, [w[:, n : n + 1] * v for w, v in zip(weights, values)])
        out = out.astype(jnp.bfloat16)
        each = size // len(outs)
        for i, ref in enumerate(outs):
            ref[:, cols] = out[i * each : i * each + each]


def combine(own, others, start, size, pieces, name):
    width = own[0].shape[1]
    piece = jax.ShapeDtypeStruct((size // pieces, width), jnp.bfloat16)
    return pl.pallas_call(
        functools.partial(combine_kernel, start=start, size=size, count=len(others)),
        out_shape=[piece] * pieces,
        in_specs=[VMEM] * (2 + len(others)),
        out_specs=[VMEM] * pieces,
        compiler_params=pltpu.CompilerParams(vmem_limit_bytes=8 * 2**20),
        name=name,
    )(*own, *others)


def place_kernel(h_ref, mine, near, far, far_near, out):
    width = near.shape[1]
    h = h_ref[0]
    pieces = (mine[...], near[...], far[:64], far_near[...])
    for j, piece in enumerate(pieces):
        out[:, pl.ds(pl.multiple_of((h ^ j) * width, HS), width)] = piece


def place(h, mine, near, far, far_near):
    return pl.pallas_call(
        place_kernel,
        out_shape=jax.ShapeDtypeStruct((64, 4 * near.shape[1]), jnp.bfloat16),
        in_specs=[SMEM] + [VMEM] * 4,
        out_specs=VMEM,
        compiler_params=pltpu.CompilerParams(vmem_limit_bytes=4 * 2**20),
        name="place",
    )(h, mine, near, far, far_near)


def local(
    image_tokens,
    shift,
    scale,
    w_query,
    w_key,
    w_value,
    q_gain,
    k_gain,
    stale_keys,
    stale_values,
    text_keys,
    text_values,
):
    rows = stale_keys.shape[0]
    piece = image_tokens.shape[0]
    head = lax.axis_index("head").astype(jnp.int32)
    h = head[None]
    order = (head ^ jnp.arange(4, dtype=jnp.int32))[:, None] * piece + jnp.arange(piece, dtype=jnp.int32)
    cos, sin = rotary(lax.axis_index("patch") * rows + order.reshape(-1))

    far_rows = across_head(2)(image_tokens)
    beside_rows = across_head(1)(image_tokens)
    pieces = [image_tokens, beside_rows, far_rows, across_head(1)(far_rows)]

    half = rows // 2
    packed = pack(stale_keys, stale_values, beside_rows)
    ways = (along_x, along_y)
    beside = [along(d)(v) for v, along in zip(packed, ways) for d in (1, 3)]
    across = [along(1)(v) for v, along in zip((beside[0], beside[2]), ways)]
    touched = touch([w_key, w_value], [beside[0]])
    near_lists = [
        join([v, *pair, far], [[(i, 0, half) for i in range(4)]], [touched], f"join_line_{g}")[0]
        for g, (v, pair, far) in enumerate(zip(packed, (beside[:2], beside[2:]), across))
    ]
    next_lists = []
    for v, along in zip(near_lists, (along_y, along_x)):
        next_lists += [along(1)(v), along(3)(v)]

    queries, fresh_keys, fresh_values = project(
        h, pieces, shift, scale, w_query, w_key, w_value, q_gain, k_gain, cos, sin
    )
    asked = {3: across_z(3)(queries), 2: across_z(2)(queries)}

    text = text_keys.shape[0]
    own = attend(
        queries,
        list(near_lists) + [text_keys, text_values, fresh_keys, fresh_values],
        [(2, 3, 0, text), (4, 5, 0, rows), (0, 0, half, 3 * half), (1, 1, half, 3 * half)],
        None,
        False,
        [],
        "attend_own_near",
    )
    halves = []
    for g in range(2):
        halves += join(
            next_lists[2 * g : 2 * g + 2],
            [[(0, 0, 2 * half)], [(1, 2 * half, 2 * half)]],
            [own[1]],
            f"join_halves_{g}",
        )
    far_lists = []
    for i, along in enumerate((along_y, along_y, along_x, along_x)):
        far_lists.append(along((1, 3)[i % 2])(halves[i]))

    def whole(arrays):
        return [(i, i, 0, v.shape[0]) for i, v in enumerate(arrays)]

    early = list(near_lists) + next_lists
    states = {3: attend(asked[3], early, whole(early), None, False, [halves[0]], "attend_early_3")}
    (query_copy,) = join([queries], [[(0, 0, rows)]], [states[3][1], asked[2]], "hold_queries")
    asked[1] = across_z(1)(query_copy)
    states[2] = attend(asked[2], early, whole(early), None, False, [query_copy], "attend_early_2")
    back, kept, after = [], [], [states[2][1]]
    for bits in (3, 2):
        part, rest = attend(
            asked[bits], far_lists, whole(far_lists), states[bits], True, after, f"attend_far_{bits}"
        )
        after = [part]
        back.append(across_z(bits)(part))
        kept.append(rest)
    every = early + far_lists
    (part,) = attend(asked[1], every, whole(every), None, True, after, "attend_all_1", True)
    back.append(across_z(1)(part))
    kept = join(kept, [[(i, 0, half)] for i in range(2)], [part], "hold_near_rows")
    rest = next_lists + far_lists
    own = attend(queries, rest, whole(rest), own, False, [kept[0]], "attend_own_rest")
    kept = [across_z(bits)(v) for bits, v in zip((3, 2), kept)]
    (far,) = combine(own, back, half, half, 1, "combine_far")
    far = across_head(2)(far)
    mine, near = combine(own, back[:2] + [back[2]] + kept + [back[2]], 0, half, 2, "combine_near")
    attended = place(h, mine, across_head(1)(near), far, across_head(1)(far[piece:]))
    return (attended, fresh_keys, fresh_values)


def solution(mesh):
    placed = (
        P(("patch", "head"), None),
        P(),
        P(),
        P(None, "head"),
        P(None, "head"),
        P(None, "head"),
        P(),
        P(),
        P("patch", "head"),
        P("patch", "head"),
        P(None, "head"),
        P(None, "head"),
    )
    return jax.shard_map(
        local,
        mesh=mesh,
        in_specs=placed,
        out_specs=(P(("patch", "head"), None), P("patch", "head"), P("patch", "head")),
        check_vma=False,
    )
```
